32 devices in a mesh: depth: 8 (over y, x, core), tile: 4 (over z).
Axes of the slice: x: 2, y: 2, z: 4, core: 2. Of those that a mesh axis runs over, the one named last changes fastest.
Arguments:
- volume: float32 [16, 512, 384], P('depth', 'tile'), may hold values from -6 to 6
- point_spread: float32 [16, 255, 255], P('depth'), may hold values from -0.005859375 to 0.005859375
- measured: float32 [512, 384], P('tile'), may hold values from -6 to 6
Outputs:
- volume_next: float32 [16, 512, 384], P('depth', 'tile')
- residual: float32 [512, 384], P('tile')
The draws below stay inside these ranges and needn't reach their ends.
All inputs are finite; a program needn't handle non-finite values.
Results may differ from the reference program's by a relative error of at most 0.0003.
Values sent between devices are 32-bit elements; how exact they have to be, the bound alone decides.
No kernel may reach another device: no remote copies, remote signals or barrier semaphores. Data moves between devices by JAX's collectives and lax.ppermute only.
A program may use at most 64 MiB of HBM per device.

```python
import jax
import jax.numpy as jnp
from jax import lax

K = 255
HALO = 127
DEPTHS = 16
NW = 384
NH = 512


def block_scale(stream_key, dims, pieces, low, top_value):
    level = 1.0
    for position, shards_of in pieces:
        heights = jax.random.uniform(jax.random.fold_in(jax.random.fold_in(stream_key, 6), position), (shards_of,), jnp.float32, low / len(pieces), top_value / len(pieces))
        level = level * jnp.repeat(jnp.exp(heights), dims[position] // shards_of).reshape((-1,) + (1,) * (len(dims) - 1 - position))
    return level


def bell_draw(own_key, extent, width, reach, split=(), dtype=jnp.bfloat16):
    entries = width * jax.random.normal(own_key, extent, jnp.float32)
    if split:
        entries = entries * block_scale(own_key, extent, split, -0.22, 0.18)
    return jnp.clip(entries, -reach, reach).astype(dtype)


def setup_inputs(seed: int = 0) -> dict:
    splits = jax.random.split(jax.random.key(seed), 4)
    return {
        "volume": bell_draw(splits[0], (DEPTHS, NH, NW), 1.0, 6.0, ((0, 8), (1, 4)), jnp.float32),
        "point_spread": bell_draw(splits[1], (DEPTHS, K, K), (K * K * DEPTHS) ** -0.5, 0.005859375, ((0, 8),), jnp.float32),
        "measured": bell_draw(splits[2], (NH, NW), 1.0, 6.0, ((0, 4),), jnp.float32),
    }


step_size = 2.0
threshold = 0.5


def reference(volume, point_spread, measured):
    height_count = measured.shape[0]
    width_count = measured.shape[1]
    shape_full = (height_count + K - 1, width_count + K - 1)

    def plane_spectrum(pair):
        plane, kernel = pair
        return jnp.fft.rfft2(plane, s=shape_full) * jnp.fft.rfft2(kernel, s=shape_full)

    total = jnp.sum(lax.map(plane_spectrum, (volume, point_spread)), axis=0)
    full_image = jnp.fft.irfft2(total, s=shape_full)
    projection = full_image[HALO:HALO + height_count, HALO:HALO + width_count].astype(jnp.float32)
    residual = projection - measured
    residual_spectrum = jnp.fft.rfft2(residual, s=shape_full)

    def plane_update(pair):
        plane, kernel = pair
        flipped = kernel[::-1, ::-1]
        back_image = jnp.fft.irfft2(residual_spectrum * jnp.fft.rfft2(flipped, s=shape_full), s=shape_full)
        gradient = back_image[HALO:HALO + height_count, HALO:HALO + width_count].astype(jnp.float32)
        shifted = plane - step_size * gradient
        return jnp.sign(shifted) * jnp.maximum(jnp.abs(shifted) - threshold, 0.0)

    volume_next = lax.map(plane_update, (volume, point_spread))
    return volume_next, residual
```

```python
import functools

import jax
import jax.numpy as jnp
import ml_dtypes
import numpy as np
from jax import lax
from jax.experimental import pallas as pl
from jax.experimental.pallas import tpu as pltpu
from jax.sharding import PartitionSpec as P

step_size = 2.0
threshold = 0.5
VMEM = pl.BlockSpec(memory_space=pltpu.VMEM)
PARAMS = pltpu.CompilerParams(vmem_limit_bytes=48 * 1024 * 1024)


def pair(table):
    high = table.astype(ml_dtypes.bfloat16)
    low = (table - high.astype(np.float64)).astype(ml_dtypes.bfloat16)
    return np.stack([high, low])


def tables(row_count, width_count, half_width):
    freq_rows = 3 * row_count
    freq_cols = -(-(width_count + half_width) // 256) * 256
    row_angle = 2.0 * np.pi / freq_rows * (np.arange(freq_rows // 2) + 0.5)
    col_angle = 2.0 * np.pi / freq_cols * (np.arange(freq_cols // 2) + 0.5)

    def rows_at(position):
        phase = row_angle[:, None] * position[None, :]
        return np.concatenate([np.cos(phase), np.sin(phase)], axis=0)

    def cols_at(position):
        phase = position[:, None] * col_angle[None, :]
        return np.concatenate([np.cos(phase), -np.sin(phase)], axis=1)

    scale = 2.0 / (freq_rows * freq_cols)
    cols = np.arange(width_count)
    frame = np.arange(freq_rows)
    row_forward = pair(rows_at(frame))
    col_forward = pair(cols_at(cols))
    row_project = pair(rows_at(frame - row_count + half_width).T * scale)
    col_project = pair(cols_at(cols + half_width).T)
    row_back = pair(rows_at(np.arange(row_count) + row_count - half_width).T * scale)
    col_back = pair(cols_at(cols - half_width).T)
    return row_forward, col_forward, row_project, col_project, row_back, col_back


def split(x):
    high = x.astype(jnp.bfloat16)
    low = (x - high.astype(jnp.float32)).astype(jnp.bfloat16)
    return high, low


def times_table(x, high, low):
    x_high, x_low = split(x)
    return jnp.dot(
        jnp.concatenate([x_high, x_low, x_high], axis=1),
        jnp.concatenate([high, high, low], axis=0),
        preferred_element_type=jnp.float32,
    )


def table_times(high, low, x):
    x_high, x_low = split(x)
    return jnp.dot(
        jnp.concatenate([high, high, low], axis=1),
        jnp.concatenate([x_high, x_low, x_high], axis=0),
        preferred_element_type=jnp.float32,
    )


def row_spectrum(high, low, x):
    q = table_times(high, low, x)
    u, v = q.shape[0] // 2, q.shape[1] // 2
    cr, ci, sr, si = q[:u, :v], q[:u, v:], q[u:, :v], q[u:, v:]
    return cr + si, ci - sr, cr - si, ci + sr


def inverse(high, low, col_high, col_low, spectrum):
    pr, pi, mr, mi = spectrum
    top = jnp.concatenate([pr + mr, pi + mi], axis=1)
    bottom = jnp.concatenate([mi - pi, pr - mr], axis=1)
    mixed = table_times(high, low, jnp.concatenate([top, bottom], axis=0))
    return times_table(mixed, col_high, col_low)


def project_kernel(
    share, volume, point_spread, measured, rf, cf, ri, ci, keep, send, optic, frame, pad
):
    planes, rows, width = volume.shape
    k = point_spread.shape[1]
    kp = pad.shape[0]
    d, t = lax.axis_index("depth"), lax.axis_index("tile")
    tiles = lax.axis_size("tile")
    total = None
    for i in range(planes):
        pad[...] = jnp.zeros_like(pad)
        pad[:k, :k] = point_spread[i]
        h = times_table(pad[...], cf[0, :kp], cf[1, :kp])
        h = row_spectrum(rf[0, :, :kp], rf[1, :, :kp], h)
        for j in range(4):
            optic[i, j] = h[j]
        f = times_table(volume[i], cf[0], cf[1])
        f = row_spectrum(rf[0, :, :rows], rf[1, :, :rows], f)
        term = (
            h[0] * f[0] - h[1] * f[1],
            h[0] * f[1] + h[1] * f[0],
            h[2] * f[2] - h[3] * f[3],
            h[2] * f[3] + h[3] * f[2],
        )
        total = term if total is None else [a + b for a, b in zip(total, term)]
    frame[...] = inverse(ri[0], ri[1], ci[0], ci[1], total)
    up = frame[:rows] * jnp.where(t == 0, 0.0, 1.0)
    own = frame[rows : 2 * rows] - measured[...] * jnp.where(d == 0, 1.0, 0.0)
    down = frame[2 * rows :] * jnp.where(t == tiles - 1, 0.0, 1.0)
    even = d % 2 == 0
    for s, strip in enumerate((up, own, down)):
        for c in range(keep.shape[0]):
            a = strip[2 * c * share : (2 * c + 1) * share]
            b = strip[(2 * c + 1) * share : (2 * c + 2) * share]
            keep[c, s] = jnp.where(even, a, b)
            send[c, s] = jnp.where(even, b, a)


def back_kernel(volume, mine, other, optic, rf, cf, ri, ci, volume_next, residual, frame):
    planes, rows, width = volume.shape
    chips, _, share, _ = mine.shape
    d = lax.axis_index("depth")
    chip, core = d // 2, d % 2
    for m in range(chips):
        c = chip ^ m
        for s in range(3):
            at = s * rows + (2 * c + core) * share
            frame[pl.ds(pl.multiple_of(at, share), share)] = mine[m, s]
            at = s * rows + (2 * c + 1 - core) * share
            frame[pl.ds(pl.multiple_of(at, share), share)] = other[m, s]
    residual[...] = frame[rows : 2 * rows]
    r = times_table(frame[...], cf[0], cf[1])
    r = row_spectrum(rf[0], rf[1], r)
    for i in range(planes):
        h = [optic[i, j] for j in range(4)]
        g = (
            h[0] * r[0] + h[1] * r[1],
            h[0] * r[1] - h[1] * r[0],
            h[2] * r[2] + h[3] * r[3],
            h[2] * r[3] - h[3] * r[2],
        )
        shifted = volume[i] - step_size * inverse(ri[0], ri[1], ci[0], ci[1], g)
        volume_next[i] = jnp.maximum(shifted - threshold, 0.0) + jnp.minimum(
            shifted + threshold, 0.0
        )


def swap(x, axis, mask):
    return lax.ppermute(x, axis, [(i, i ^ mask) for i in range(lax.axis_size(axis))])


def both_ways(pairs):
    return [(a, b) for a, b in pairs] + [(b, a) for a, b in pairs]


def neighbours(parts):
    up, own, down = parts[0], parts[1], parts[2]
    t, n = lax.axis_index("tile"), lax.axis_size("tile")
    for_above, for_below = parts[1:], parts[:2]
    even = t % 2 == 0
    first = both_ways([(i, i + 1) for i in range(0, n - 1, 2)])
    second = both_ways([(i, i + 1) for i in range(1, n - 1, 2)])
    a = lax.ppermute(jnp.where(even, for_above, for_below), "tile", first)
    b = lax.ppermute(jnp.where(even, for_below, for_above), "tile", second)
    lower = t % 4 < 2
    third = both_ways([(i, i + 2) for i in range(n - 2) if i % 4 < 2])
    fourth = both_ways([(i, i + 2) for i in range(n - 2) if i % 4 >= 2])
    c = lax.ppermute(jnp.where(lower, down, up), "tile", third)
    e = jnp.zeros_like(c)
    if fourth:
        e = lax.ppermute(jnp.where(lower, up, down), "tile", fourth)
    from_above = jnp.where(even, a, b)
    from_below = jnp.where(even, b, a)
    far_above = jnp.where(lower, c, e)
    far_below = jnp.where(lower, e, c)
    return jnp.stack(
        [
            from_below[0] + up + far_below,
            own + from_below[1] + from_above[0],
            from_above[1] + down + far_above,
        ]
    )


def per_device(volume, point_spread, measured):
    planes, rows, width = volume.shape
    half_width = (point_spread.shape[1] - 1) // 2
    n = lax.axis_size("depth")
    chips = n // 2
    share = rows // n
    f32 = jnp.float32
    rf, cf, rp, cp, rb, cb = (
        jnp.asarray(x) for x in tables(rows, width, half_width)
    )
    half = (chips, 3, share, width)
    padded = -(-point_spread.shape[1] // 128) * 128
    keep, send, optic = pl.pallas_call(
        functools.partial(project_kernel, share),
        out_shape=[
            jax.ShapeDtypeStruct(half, f32),
            jax.ShapeDtypeStruct(half, f32),
            jax.ShapeDtypeStruct((planes, 4, rf.shape[1] // 2, cf.shape[2] // 2), f32),
        ],
        in_specs=[VMEM] * 7,
        out_specs=[VMEM] * 3,
        scratch_shapes=[
            pltpu.VMEM((3 * rows, width), f32),
            pltpu.VMEM((padded, padded), f32),
        ],
        compiler_params=PARAMS,
        name="project",
    )(volume, point_spread, measured, rf, cf, rp, cp)
    halves = keep + swap(send, "depth", 1)
    chip = lax.axis_index("depth") // 2
    mine = [lax.dynamic_index_in_dim(halves, chip ^ m, 0, False) for m in range(chips)]
    parts = mine[0]
    arrived = [swap(mine[m], "depth", 2 * m) for m in range(1, chips)]
    for x in arrived:
        parts = parts + x
    strips = neighbours(parts)
    gathered = jnp.stack([strips] + [swap(strips, "depth", 2 * m) for m in range(1, chips)])
    other = swap(gathered, "depth", 1)
    volume_next, residual = pl.pallas_call(
        back_kernel,
        out_shape=[
            jax.ShapeDtypeStruct(volume.shape, f32),
            jax.ShapeDtypeStruct(measured.shape, f32),
        ],
        in_specs=[VMEM] * 8,
        out_specs=[VMEM] * 2,
        scratch_shapes=[pltpu.VMEM((3 * rows, width), f32)],
        compiler_params=PARAMS,
        name="back",
    )(volume, gathered, other, optic, rf, cf, rb, cb)
    return volume_next, residual


def solution(mesh):
    placed = (P("depth", "tile", None), P("depth", None, None), P("tile", None))
    return jax.shard_map(
        per_device,
        mesh=mesh,
        in_specs=placed,
        out_specs=(P("depth", "tile", None), P("tile", None)),
        check_vma=False,
    )
```

```python
import functools

import jax
import jax.numpy as jnp
import ml_dtypes
import numpy as np
from jax import lax
from jax.experimental import pallas as pl
from jax.experimental.pallas import tpu as pltpu
from jax.sharding import PartitionSpec as P

step_size = 2.0
threshold = 0.5
VMEM = pl.BlockSpec(memory_space=pltpu.VMEM)
PARAMS = pltpu.CompilerParams(vmem_limit_bytes=24 * 1024 * 1024)
SMALL = pltpu.CompilerParams(vmem_limit_bytes=4 * 1024 * 1024)


def pair(table):
    high = table.astype(ml_dtypes.bfloat16)
    low = (table - high.astype(np.float64)).astype(ml_dtypes.bfloat16)
    return np.stack([high, low])


def tables(row_count, width_count, half_width):
    freq_rows = 3 * row_count
    freq_cols = -(-(width_count + half_width) // 256) * 256
    row_angle = 2.0 * np.pi / freq_rows * (np.arange(freq_rows // 2) + 0.5)
    col_angle = 2.0 * np.pi / freq_cols * (np.arange(freq_cols // 2) + 0.5)

    def rows_at(position):
        phase = row_angle[:, None] * position[None, :]
        return np.concatenate([np.cos(phase), np.sin(phase)], axis=0)

    def cols_at(position):
        phase = position[:, None] * col_angle[None, :]
        return np.concatenate([np.cos(phase), -np.sin(phase)], axis=1)

    scale = 2.0 / (freq_rows * freq_cols)
    cols = np.arange(width_count)
    frame = np.arange(freq_rows)
    row_forward = pair(rows_at(frame))
    col_forward = pair(cols_at(cols))
    row_project = pair(rows_at(frame - row_count + half_width).T * scale)
    col_project = pair(cols_at(cols + half_width).T)
    row_back = pair(rows_at(np.arange(row_count) + row_count - half_width).T * scale)
    col_back = pair(cols_at(cols - half_width).T)
    return row_forward, col_forward, row_project, col_project, row_back, col_back


def split(x):
    high = x.astype(jnp.bfloat16)
    low = (x - high.astype(jnp.float32)).astype(jnp.bfloat16)
    return high, low


def times_table(x, high, low):
    x_high, x_low = split(x)
    return jnp.dot(
        jnp.concatenate([x_high, x_low, x_high], axis=1),
        jnp.concatenate([high, high, low], axis=0),
        preferred_element_type=jnp.float32,
    )


def table_times(high, low, x):
    x_high, x_low = split(x)
    return jnp.dot(
        jnp.concatenate([high, high, low], axis=1),
        jnp.concatenate([x_high, x_low, x_high], axis=0),
        preferred_element_type=jnp.float32,
    )


def row_spectrum(high, low, x):
    q = table_times(high, low, x)
    u, v = q.shape[0] // 2, q.shape[1] // 2
    cr, ci, sr, si = q[:u, :v], q[:u, v:], q[u:, :v], q[u:, v:]
    return cr + si, ci - sr, cr - si, ci + sr


def inverse(high, low, col_high, col_low, spectrum):
    pr, pi, mr, mi = spectrum
    top = jnp.concatenate([pr + mr, pi + mi], axis=1)
    bottom = jnp.concatenate([mi - pi, pr - mr], axis=1)
    mixed = table_times(high, low, jnp.concatenate([top, bottom], axis=0))
    return times_table(mixed, col_high, col_low)


def project_kernel(
    share,
    volume_h,
    point_spread_h,
    measured_h,
    rf_h,
    cf_h,
    ri_h,
    ci_h,
    keep,
    send,
    optic,
    volume,
    point_spread,
    measured,
    rf,
    cf,
    ri,
    ci,
    frame,
    pad,
    arrived,
):
    moves = {}
    order = (
        ("spread", point_spread_h, point_spread),
        ("cf", cf_h, cf),
        ("rf", rf_h, rf),
        ("volume", volume_h, volume),
        ("ri", ri_h, ri),
        ("ci", ci_h, ci),
        ("measured", measured_h, measured),
    )
    for i, (name, source, target) in enumerate(order):
        moves[name] = pltpu.make_async_copy(source, target, arrived.at[i])
        moves[name].start()
    planes, rows, width = volume.shape
    k = point_spread.shape[0]
    kp = pad.shape[1]
    d, t = lax.axis_index("depth"), lax.axis_index("tile")
    tiles = lax.axis_size("tile")
    pad[...] = jnp.zeros_like(pad)
    moves["spread"].wait()
    for i in range(planes):
        pad[i, :k, :k] = point_spread[:, i, :]
    moves["cf"].wait()
    spread = [times_table(pad[i], cf[0, :kp], cf[1, :kp]) for i in range(planes)]
    moves["volume"].wait()
    image = [times_table(volume[i], cf[0], cf[1]) for i in range(planes)]
    moves["rf"].wait()
    total = None
    for i in range(planes):
        h = row_spectrum(rf[0, :, :kp], rf[1, :, :kp], spread[i])
        for j in range(4):
            optic[i, j] = h[j]
        f = row_spectrum(rf[0, :, :rows], rf[1, :, :rows], image[i])
        term = (
            h[0] * f[0] - h[1] * f[1],
            h[0] * f[1] + h[1] * f[0],
            h[2] * f[2] - h[3] * f[3],
            h[2] * f[3] + h[3] * f[2],
        )
        total = term if total is None else [a + b for a, b in zip(total, term)]
    moves["ri"].wait()
    moves["ci"].wait()
    frame[...] = inverse(ri[0], ri[1], ci[0], ci[1], total)
    moves["measured"].wait()
    up = frame[:rows] * jnp.where(t == 0, 0.0, 1.0)
    own = frame[rows : 2 * rows] - measured[...] * jnp.where(d == 0, 1.0, 0.0)
    down = frame[2 * rows :] * jnp.where(t == tiles - 1, 0.0, 1.0)
    even = d % 2 == 0
    for s, strip in enumerate((up, own, down)):
        for c in range(keep.shape[0]):
            a = strip[2 * c * share : (2 * c + 1) * share]
            b = strip[(2 * c + 1) * share : (2 * c + 2) * share]
            keep[c, s] = jnp.where(even, a, b)
            send[c, s] = jnp.where(even, b, a)


def first_sum_kernel(keep, received, *outs):
    chip = lax.axis_index("depth") // 2
    for m, out in enumerate(outs):
        out[...] = keep[chip ^ m] + received[chip ^ m]


def second_sum_kernel(fourth, own, *refs):
    ins, outs = refs[: len(refs) - (4 + fourth)], refs[len(refs) - (4 + fourth) :]
    t = lax.axis_index("tile")
    even, lower = t % 2 == 0, t % 4 < 2
    parts = own[...]
    for x in ins:
        parts = parts + x[...]
    outs[0][...] = parts
    outs[1][...] = jnp.where(even, parts[1:], parts[:2])
    outs[2][...] = jnp.where(even, parts[:2], parts[1:])
    outs[3][...] = jnp.where(lower, parts[2], parts[0])
    if fourth:
        outs[4][...] = jnp.where(lower, parts[0], parts[2])


def third_sum_kernel(parts, a, b, c, *refs):
    strips = refs[-1]
    t = lax.axis_index("tile")
    even, lower = t % 2 == 0, t % 4 < 2
    e = refs[0][...] if len(refs) > 1 else jnp.zeros_like(c)
    from_above = jnp.where(even, a[...], b[...])
    from_below = jnp.where(even, b[...], a[...])
    strips[0] = from_below[0] + parts[0] + jnp.where(lower, e, c[...])
    strips[1] = parts[1] + from_below[1] + from_above[0]
    strips[2] = from_above[1] + parts[2] + jnp.where(lower, c[...], e)


def stack_kernel(*refs):
    for m, x in enumerate(refs[:-1]):
        refs[-1][m] = x[...]


def back_kernel(volume, mine, other, optic, rf, cf, ri, ci, volume_next, residual, frame):
    planes, rows, width = volume.shape
    chips, _, share, _ = mine.shape
    d = lax.axis_index("depth")
    chip, core = d // 2, d % 2
    for m in range(chips):
        c = chip ^ m
        for s in range(3):
            at = s * rows + (2 * c + core) * share
            frame[pl.ds(pl.multiple_of(at, share), share)] = mine[m, s]
            at = s * rows + (2 * c + 1 - core) * share
            frame[pl.ds(pl.multiple_of(at, share), share)] = other[m, s]
    residual[...] = frame[rows : 2 * rows]
    r = times_table(frame[...], cf[0], cf[1])
    r = row_spectrum(rf[0], rf[1], r)
    for i in range(planes):
        h = [optic[i, j] for j in range(4)]
        g = (
            h[0] * r[0] + h[1] * r[1],
            h[0] * r[1] - h[1] * r[0],
            h[2] * r[2] + h[3] * r[3],
            h[2] * r[3] - h[3] * r[2],
        )
        shifted = volume[i] - step_size * inverse(ri[0], ri[1], ci[0], ci[1], g)
        volume_next[i] = jnp.maximum(shifted - threshold, 0.0) + jnp.minimum(
            shifted + threshold, 0.0
        )


def swap(x, axis, mask):
    return lax.ppermute(x, axis, [(i, i ^ mask) for i in range(lax.axis_size(axis))])


def both_ways(pairs):
    return [(a, b) for a, b in pairs] + [(b, a) for a, b in pairs]


def local(kernel, name, outs, *args):
    return pl.pallas_call(
        kernel,
        out_shape=[pltpu.VMEM(x, jnp.float32) for x in outs],
        in_specs=[VMEM] * len(args),
        out_specs=[VMEM] * len(outs),
        compiler_params=SMALL,
        name=name,
    )(*args)


def per_device(volume, point_spread, measured):
    planes, rows, width = volume.shape
    half_width = (point_spread.shape[1] - 1) // 2
    n = lax.axis_size("depth")
    tiles = lax.axis_size("tile")
    chips = n // 2
    share = rows // n
    f32 = jnp.float32
    rf, cf, rp, cp, rb, cb = (
        jnp.asarray(x) for x in tables(rows, width, half_width)
    )
    half = (chips, 3, share, width)
    piece = (3, share, width)
    kp = -(-point_spread.shape[1] // 128) * 128
    spread = jnp.transpose(point_spread, (1, 0, 2))
    operands = (volume, spread, measured, rf, cf, rp, cp)
    keep, send, optic = pl.pallas_call(
        functools.partial(project_kernel, share),
        out_shape=[
            pltpu.VMEM(half, f32),
            pltpu.VMEM(half, f32),
            pltpu.VMEM((planes, 4, rf.shape[1] // 2, cf.shape[2] // 2), f32),
        ],
        in_specs=[pl.BlockSpec(memory_space=pltpu.HBM)] * 7,
        out_specs=[VMEM] * 3,
        scratch_shapes=[pltpu.VMEM(x.shape, x.dtype) for x in operands]
        + [
            pltpu.VMEM((3 * rows, width), f32),
            pltpu.VMEM((planes, kp, kp), f32),
            pltpu.SemaphoreType.DMA((7,)),
        ],
        compiler_params=PARAMS,
        name="project",
    )(*[pltpu.with_memory_space_constraint(x, pltpu.HBM) for x in operands])
    received = swap(send, "depth", 1)
    mine = local(first_sum_kernel, "first_sum", [piece] * chips, keep, received)
    arrived = [swap(mine[m], "depth", 2 * m) for m in range(1, chips)]
    pairs = [
        [(i, i + 1) for i in range(0, tiles - 1, 2)],
        [(i, i + 1) for i in range(1, tiles - 1, 2)],
        [(i, i + 2) for i in range(tiles - 2) if i % 4 < 2],
        [(i, i + 2) for i in range(tiles - 2) if i % 4 >= 2],
    ]
    fourth = int(bool(pairs[3]))
    edge = (2, share, width)
    parts, *sends = local(
        functools.partial(second_sum_kernel, fourth),
        "second_sum",
        [piece, edge, edge] + [piece[1:]] * (1 + fourth),
        mine[0],
        *arrived,
    )
    arrived = [lax.ppermute(x, "tile", both_ways(p)) for x, p in zip(sends, pairs)]
    (strips,) = local(third_sum_kernel, "third_sum", [piece], parts, *arrived)
    arrived = [swap(strips, "depth", 2 * m) for m in range(1, chips)]
    (gathered,) = local(stack_kernel, "stack", [half], strips, *arrived)
    other = swap(gathered, "depth", 1)
    volume_next, residual = pl.pallas_call(
        back_kernel,
        out_shape=[
            jax.ShapeDtypeStruct(volume.shape, f32),
            jax.ShapeDtypeStruct(measured.shape, f32),
        ],
        in_specs=[VMEM] * 8,
        out_specs=[VMEM] * 2,
        scratch_shapes=[pltpu.VMEM((3 * rows, width), f32)],
        compiler_params=PARAMS,
        name="back",
    )(volume, gathered, other, optic, rf, cf, rb, cb)
    return volume_next, residual


def solution(mesh):
    placed = (P("depth", "tile", None), P("depth", None, None), P("tile", None))
    return jax.shard_map(
        per_device,
        mesh=mesh,
        in_specs=placed,
        out_specs=(P("depth", "tile", None), P("tile", None)),
        check_vma=False,
    )
```

```python
import jax
import jax.numpy as jnp
import ml_dtypes
import numpy as np
from jax import lax
from jax.experimental import pallas as pl
from jax.experimental.pallas import tpu as pltpu
from jax.sharding import PartitionSpec as P

step_size = 2.0
threshold = 0.5
VMEM = pl.BlockSpec(memory_space=pltpu.VMEM)
PARAMS = pltpu.CompilerParams(vmem_limit_bytes=24 * 1024 * 1024)
SMALL = pltpu.CompilerParams(vmem_limit_bytes=4 * 1024 * 1024)


def pair(table):
    high = table.astype(ml_dtypes.bfloat16)
    low = (table - high.astype(np.float64)).astype(ml_dtypes.bfloat16)
    return np.stack([high, low])


def tables(row_count, width_count, half_width):
    freq_rows = 3 * row_count
    freq_cols = -(-(width_count + half_width) // 256) * 256
    row_angle = 2.0 * np.pi / freq_rows * (np.arange(freq_rows // 2) + 0.5)
    col_angle = 2.0 * np.pi / freq_cols * (np.arange(freq_cols // 2) + 0.5)

    def rows_at(position):
        phase = row_angle[:, None] * position[None, :]
        return np.concatenate([np.cos(phase), np.sin(phase)], axis=0)

    def cols_at(position):
        phase = position[:, None] * col_angle[None, :]
        return np.concatenate([np.cos(phase), -np.sin(phase)], axis=1)

    scale = 2.0 / (freq_rows * freq_cols)
    cols = np.arange(width_count)
    frame = np.arange(freq_rows)
    row_forward = pair(rows_at(frame))
    col_forward = pair(cols_at(cols))
    row_project = pair(rows_at(frame - row_count + half_width).T * scale)
    col_project = pair(cols_at(cols + half_width).T)
    row_back = pair(rows_at(np.arange(row_count) + row_count - half_width).T * scale)
    col_back = pair(cols_at(cols - half_width).T)
    return row_forward, col_forward, row_project, col_project, row_back, col_back


def split(x):
    high = x.astype(jnp.bfloat16)
    low = (x - high.astype(jnp.float32)).astype(jnp.bfloat16)
    return high, low


def times_table(x, high, low):
    x_high, x_low = split(x)
    return jnp.dot(
        jnp.concatenate([x_high, x_low, x_high], axis=1),
        jnp.concatenate([high, high, low], axis=0),
        preferred_element_type=jnp.float32,
    )


def table_times(high, low, x):
    x_high, x_low = split(x)
    return jnp.dot(
        jnp.concatenate([high, high, low], axis=1),
        jnp.concatenate([x_high, x_low, x_high], axis=0),
        preferred_element_type=jnp.float32,
    )


def row_spectrum(high, low, x):
    q = table_times(high, low, x)
    u, v = q.shape[0] // 2, q.shape[1] // 2
    cr, ci, sr, si = q[:u, :v], q[:u, v:], q[u:, :v], q[u:, v:]
    return cr + si, ci - sr, cr - si, ci + sr


def inverse(high, low, col_high, col_low, spectrum):
    pr, pi, mr, mi = spectrum
    top = jnp.concatenate([pr + mr, pi + mi], axis=1)
    bottom = jnp.concatenate([mi - pi, pr - mr], axis=1)
    mixed = table_times(high, low, jnp.concatenate([top, bottom], axis=0))
    return times_table(mixed, col_high, col_low)


def project_kernel(
    volume_h,
    point_spread_h,
    measured_h,
    rf_h,
    cf_h,
    ri_h,
    ci_h,
    keep,
    send,
    optic,
    volume,
    point_spread,
    measured,
    rf,
    cf,
    ri,
    ci,
    frame,
    pad,
    arrived,
):
    moves = {}
    order = (
        ("spread", point_spread_h, point_spread),
        ("cf", cf_h, cf),
        ("rf", rf_h, rf),
        ("volume", volume_h, volume),
        ("ri", ri_h, ri),
        ("ci", ci_h, ci),
        ("measured", measured_h, measured),
    )
    for i, (name, source, target) in enumerate(order):
        moves[name] = pltpu.make_async_copy(source, target, arrived.at[i])
        moves[name].start()
    planes, rows, width = volume.shape
    k = point_spread.shape[0]
    kp = pad.shape[1]
    d, t = lax.axis_index("depth"), lax.axis_index("tile")
    tiles = lax.axis_size("tile")
    pad[...] = jnp.zeros_like(pad)
    moves["spread"].wait()
    for i in range(planes):
        pad[i, :k, :k] = point_spread[:, i, :]
    moves["cf"].wait()
    spread = [times_table(pad[i], cf[0, :kp], cf[1, :kp]) for i in range(planes)]
    moves["volume"].wait()
    image = [times_table(volume[i], cf[0], cf[1]) for i in range(planes)]
    moves["rf"].wait()
    total = None
    for i in range(planes):
        h = row_spectrum(rf[0, :, :kp], rf[1, :, :kp], spread[i])
        for j in range(4):
            optic[i, j] = h[j]
        f = row_spectrum(rf[0, :, :rows], rf[1, :, :rows], image[i])
        term = (
            h[0] * f[0] - h[1] * f[1],
            h[0] * f[1] + h[1] * f[0],
            h[2] * f[2] - h[3] * f[3],
            h[2] * f[3] + h[3] * f[2],
        )
        total = term if total is None else [a + b for a, b in zip(total, term)]
    moves["ri"].wait()
    moves["ci"].wait()
    frame[...] = inverse(ri[0], ri[1], ci[0], ci[1], total)
    moves["measured"].wait()
    up = frame[:rows] * jnp.where(t == 0, 0.0, 1.0)
    own = frame[rows : 2 * rows] - measured[...] * jnp.where(d == 0, 1.0, 0.0)
    down = frame[2 * rows :] * jnp.where(t == tiles - 1, 0.0, 1.0)
    even = d % 2 == 0
    half = rows // 2
    for s, strip in enumerate((up, own, down)):
        keep[s] = jnp.where(even, strip[:half], strip[half:])
        send[s] = jnp.where(even, strip[half:], strip[:half])


def split_kernel(keep, received, own, first, second):
    even = lax.axis_index("tile") % 2 == 0
    up, down = keep[0] + received[0], keep[2] + received[2]
    own[...] = keep[1] + received[1]
    first[...] = jnp.where(even, down, up)
    second[...] = jnp.where(even, up, down)


def tree(terms):
    if len(terms) == 1:
        return terms[0]
    middle = len(terms) // 2
    return tree(terms[:middle]) + tree(terms[middle:])


def paired():
    t, n = lax.axis_index("tile"), lax.axis_size("tile")
    even = t % 2 == 0
    first = jnp.where(even, t + 1, t - 1)
    second = jnp.where(even, t - 1, t + 1)
    return first < n, jnp.logical_and(second >= 0, second < n)


def tile_sum_kernel(own, a, b, out):
    first, second = paired()
    out[...] = own[...] + jnp.where(first, a[...], 0.0) + jnp.where(second, b[...], 0.0)


def sum_kernel(*refs):
    refs[-1][...] = tree([x[...] for x in refs[:-1]])


def stack_kernel(*refs):
    for m, x in enumerate(refs[:-1]):
        refs[-1][m] = x[...]


def back_kernel(volume, mine, other, optic, rf, cf, ri, ci, volume_next, residual, frame):
    planes, rows, width = volume.shape
    half = rows // 2
    core = lax.axis_index("depth") % 2
    even = lax.axis_index("tile") % 2 == 0
    strips = (1, jnp.where(even, 2, 0), jnp.where(even, 0, 2))
    for m, (strip, valid) in enumerate(zip(strips, (True,) + paired())):
        at = strip * rows + core * half
        frame[pl.ds(pl.multiple_of(at, half), half)] = jnp.where(valid, mine[m], 0.0)
        at = strip * rows + (1 - core) * half
        frame[pl.ds(pl.multiple_of(at, half), half)] = jnp.where(valid, other[m], 0.0)
    residual[...] = frame[rows : 2 * rows]
    r = times_table(frame[...], cf[0], cf[1])
    r = row_spectrum(rf[0], rf[1], r)
    for i in range(planes):
        h = [optic[i, j] for j in range(4)]
        g = (
            h[0] * r[0] + h[1] * r[1],
            h[0] * r[1] - h[1] * r[0],
            h[2] * r[2] + h[3] * r[3],
            h[2] * r[3] - h[3] * r[2],
        )
        shifted = volume[i] - step_size * inverse(ri[0], ri[1], ci[0], ci[1], g)
        volume_next[i] = jnp.maximum(shifted - threshold, 0.0) + jnp.minimum(
            shifted + threshold, 0.0
        )


def swap(x, axis, mask):
    return lax.ppermute(x, axis, [(i, i ^ mask) for i in range(lax.axis_size(axis))])


def pairing(depths, tiles, start):
    partner = {}
    for t in range(tiles):
        other = t + 1 if (t - start) % 2 == 0 else t - 1
        for d in range(depths):
            inside = 0 <= other < tiles
            partner[d * tiles + t] = d * tiles + other if inside else (d ^ 1) * tiles + t
    return sorted(partner.items())


def local(kernel, name, outs, *args):
    return pl.pallas_call(
        kernel,
        out_shape=[pltpu.VMEM(x, jnp.float32) for x in outs],
        in_specs=[VMEM] * len(args),
        out_specs=[VMEM] * len(outs),
        compiler_params=SMALL,
        name=name,
    )(*args)


def per_device(volume, point_spread, measured):
    planes, rows, width = volume.shape
    half_width = (point_spread.shape[1] - 1) // 2
    n = lax.axis_size("depth")
    tiles = lax.axis_size("tile")
    chips = n // 2
    f32 = jnp.float32
    rf, cf, rp, cp, rb, cb = (
        jnp.asarray(x) for x in tables(rows, width, half_width)
    )
    half = (3, rows // 2, width)
    piece = (rows // 2, width)
    kp = -(-point_spread.shape[1] // 128) * 128
    spread = jnp.transpose(point_spread, (1, 0, 2))
    operands = (volume, spread, measured, rf, cf, rp, cp)
    keep, send, optic = pl.pallas_call(
        project_kernel,
        out_shape=[
            pltpu.VMEM(half, f32),
            pltpu.VMEM(half, f32),
            pltpu.VMEM((planes, 4, rf.shape[1] // 2, cf.shape[2] // 2), f32),
        ],
        in_specs=[pl.BlockSpec(memory_space=pltpu.HBM)] * 7,
        out_specs=[VMEM] * 3,
        scratch_shapes=[pltpu.VMEM(x.shape, x.dtype) for x in operands]
        + [
            pltpu.VMEM((3 * rows, width), f32),
            pltpu.VMEM((planes, kp, kp), f32),
            pltpu.SemaphoreType.DMA((7,)),
        ],
        compiler_params=PARAMS,
        name="project",
    )(*[pltpu.with_memory_space_constraint(x, pltpu.HBM) for x in operands])
    received = swap(send, "depth", 1)
    pairs = [pairing(n, tiles, start) for start in (0, 1)]
    own, *sends = local(split_kernel, "split", [piece] * 3, keep, received)
    beside = [lax.ppermute(x, ("depth", "tile"), p) for x, p in zip(sends, pairs)]
    (part,) = local(tile_sum_kernel, "sum_tiles", [piece], own, *beside)
    others = [swap(part, "depth", 2 * m) for m in range(1, chips)]
    (whole,) = local(sum_kernel, "sum_chips", [piece], part, *others)
    beside = [lax.ppermute(whole, ("depth", "tile"), p) for p in pairs]
    (gathered,) = local(stack_kernel, "stack", [half], whole, *beside)
    other = swap(gathered, "depth", 1)
    volume_next, residual = pl.pallas_call(
        back_kernel,
        out_shape=[
            jax.ShapeDtypeStruct(volume.shape, f32),
            jax.ShapeDtypeStruct(measured.shape, f32),
        ],
        in_specs=[VMEM] * 8,
        out_specs=[VMEM] * 2,
        scratch_shapes=[pltpu.VMEM((3 * rows, width), f32)],
        compiler_params=PARAMS,
        name="back",
    )(volume, gathered, other, optic, rf, cf, rb, cb)
    return volume_next, residual


def solution(mesh):
    placed = (P("depth", "tile", None), P("depth", None, None), P("tile", None))
    return jax.shard_map(
        per_device,
        mesh=mesh,
        in_specs=placed,
        out_specs=(P("depth", "tile", None), P("tile", None)),
        check_vma=False,
    )
```

```python
import jax
import jax.numpy as jnp
import ml_dtypes
import numpy as np
from jax import lax
from jax.experimental import pallas as pl
from jax.experimental.pallas import tpu as pltpu
from jax.sharding import PartitionSpec as P

step_size = 2.0
threshold = 0.5
VMEM = pl.BlockSpec(memory_space=pltpu.VMEM)
HBM = pl.BlockSpec(memory_space=pltpu.HBM)
PARAMS = pltpu.CompilerParams(vmem_limit_bytes=24 * 1024 * 1024)
SMALL = pltpu.CompilerParams(vmem_limit_bytes=4 * 1024 * 1024)


def pair(table):
    high = table.astype(ml_dtypes.bfloat16)
    low = (table - high.astype(np.float64)).astype(ml_dtypes.bfloat16)
    return np.stack([high, low])


def tables(row_count, width_count, half_width):
    freq_rows = 3 * row_count
    freq_cols = -(-(width_count + half_width) // 256) * 256
    row_angle = 2.0 * np.pi / freq_rows * (np.arange(freq_rows // 2) + 0.5)
    col_angle = 2.0 * np.pi / freq_cols * (np.arange(freq_cols // 2) + 0.5)
    row_phase = row_angle[:, None] * np.arange(freq_rows)[None, :]
    col_phase = np.arange(width_count)[:, None] * col_angle[None, :]
    row_table = np.concatenate([np.cos(row_phase), np.sin(row_phase)], axis=0)
    col_table = np.concatenate([np.cos(col_phase), -np.sin(col_phase)], axis=1)
    centre = np.stack([np.cos(half_width * col_angle), np.sin(half_width * col_angle)])
    shift = np.zeros((8, freq_cols // 2), np.float32)
    shift[:2] = centre * (2.0 / (freq_rows * freq_cols))
    return pair(row_table), pair(col_table), shift


def split(x):
    high = x.astype(jnp.bfloat16)
    low = (x - high.astype(jnp.float32)).astype(jnp.bfloat16)
    return high, low


def times_table(x, high, low):
    x_high, x_low = split(x)
    return jnp.dot(
        jnp.concatenate([x_high, x_low, x_high], axis=1),
        jnp.concatenate([high, high, low], axis=0),
        preferred_element_type=jnp.float32,
    )


def table_times(high, low, x):
    x_high, x_low = split(x)
    return jnp.dot(
        jnp.concatenate([high, high, low], axis=1),
        jnp.concatenate([x_high, x_low, x_high], axis=0),
        preferred_element_type=jnp.float32,
    )


def row_spectrum(high, low, x):
    q = table_times(high, low, x)
    u, v = q.shape[0] // 2, q.shape[1] // 2
    cr, ci, sr, si = q[:u, :v], q[:u, v:], q[u:, :v], q[u:, v:]
    return cr + si, ci - sr, cr - si, ci + sr


def folded(spectrum):
    pr, pi, mr, mi = spectrum
    top = jnp.concatenate([pr + mr, pi + mi], axis=1)
    bottom = jnp.concatenate([mi - pi, pr - mr], axis=1)
    return jnp.concatenate([top, bottom], axis=0)


def project_kernel(
    volume_h,
    point_spread_h,
    rf_h,
    cf_h,
    shift_h,
    measured_h,
    keep,
    send,
    optic,
    rf,
    rt,
    cf,
    ct,
    volume,
    point_spread,
    shift,
    measured,
    pad,
    arrived,
):
    kp = pad.shape[1]
    moves = {}
    order = (
        ("spread", point_spread_h, point_spread),
        ("cf", cf_h.at[:, :kp], cf.at[:, :kp]),
        ("shift", shift_h, shift),
        ("rf", rf_h, rf),
        ("volume", volume_h, volume),
        ("cf_rest", cf_h.at[:, kp:], cf.at[:, kp:]),
        ("measured", measured_h, measured),
    )
    for i, (name, source, target) in enumerate(order):
        moves[name] = pltpu.make_async_copy(source, target, arrived.at[i])
        moves[name].start()
    planes, rows, width = volume.shape
    k = point_spread.shape[0]
    d, t = lax.axis_index("depth"), lax.axis_index("tile")
    tiles = lax.axis_size("tile")
    above = rows - (k - 1) // 2
    pad[...] = jnp.zeros_like(pad)
    moves["spread"].wait()
    for i in range(planes):
        pad[i, above : above + k, :k] = point_spread[:, i, :]
    moves["cf"].wait()
    moves["shift"].wait()
    cos, sin = shift[0:1], shift[1:2]
    v = cos.shape[1]
    x = times_table(pad[...].reshape(planes * kp, kp), cf[0, :kp], cf[1, :kp])
    re, im = x[:, :v], x[:, v:]
    spread = jnp.concatenate([re * cos - im * sin, re * sin + im * cos], axis=1)
    moves["volume"].wait()
    moves["cf_rest"].wait()
    image = times_table(volume[...].reshape(planes * rows, width), cf[0], cf[1])
    for i in range(2):
        ct[i] = cf[i].T
    moves["rf"].wait()
    rt[0] = rf[0].T
    rt[1] = rf[1].T
    total = None
    for i in range(planes):
        h = row_spectrum(rf[0, :, :kp], rf[1, :, :kp], spread[i * kp : (i + 1) * kp])
        for j in range(4):
            optic[i, j] = h[j]
        f = row_spectrum(rf[0, :, :rows], rf[1, :, :rows], image[i * rows : (i + 1) * rows])
        term = (
            h[0] * f[0] - h[1] * f[1],
            h[0] * f[1] + h[1] * f[0],
            h[2] * f[2] - h[3] * f[3],
            h[2] * f[3] + h[3] * f[2],
        )
        total = term if total is None else [a + b for a, b in zip(total, term)]
    frame = times_table(table_times(rt[0], rt[1], folded(total)), ct[0], ct[1])
    moves["measured"].wait()
    strips = (
        frame[:rows] * jnp.where(t == 0, 0.0, 1.0),
        frame[rows : 2 * rows] - measured[...] * jnp.where(d == 0, 1.0, 0.0),
        frame[2 * rows :] * jnp.where(t == tiles - 1, 0.0, 1.0),
    )
    half = rows // 2
    for j, strip in enumerate(strips):
        keep[j] = jnp.where(d % 2 == 0, strip[:half], strip[half:])
        send[j] = jnp.where(d % 2 == 0, strip[half:], strip[:half])


def split_kernel(keep, received, own, first, second):
    even = lax.axis_index("tile") % 2 == 0
    up, down = keep[0] + received[0], keep[2] + received[2]
    own[...] = keep[1] + received[1]
    first[...] = jnp.where(even, down, up)
    second[...] = jnp.where(even, up, down)


def tree(terms):
    if len(terms) == 1:
        return terms[0]
    middle = len(terms) // 2
    return tree(terms[:middle]) + tree(terms[middle:])


def paired():
    t, n = lax.axis_index("tile"), lax.axis_size("tile")
    even = t % 2 == 0
    first = jnp.where(even, t + 1, t - 1)
    second = jnp.where(even, t - 1, t + 1)
    return first < n, jnp.logical_and(second >= 0, second < n)


def tile_sum_kernel(own, a, b, out):
    first, second = paired()
    out[...] = own[...] + jnp.where(first, a[...], 0.0) + jnp.where(second, b[...], 0.0)


def sum_kernel(*refs):
    refs[-1][...] = tree([x[...] for x in refs[:-1]])


def stack_kernel(*refs):
    for m, x in enumerate(refs[:-1]):
        refs[-1][m] = x[...]


def back_kernel(volume, mine, other, optic, rf, rt, cf, ct, volume_next, residual, frame):
    planes, rows, width = volume.shape
    half = rows // 2
    core = lax.axis_index("depth") % 2
    even = lax.axis_index("tile") % 2 == 0
    first, second = paired()
    strips = ((1, True), (jnp.where(even, 0, 2), second), (jnp.where(even, 2, 0), first))
    for m, (strip, valid) in enumerate(strips):
        at = strip * rows + core * half
        frame[pl.ds(pl.multiple_of(at, half), half)] = jnp.where(valid, mine[m], 0.0)
        at = strip * rows + (1 - core) * half
        frame[pl.ds(pl.multiple_of(at, half), half)] = jnp.where(valid, other[m], 0.0)
    residual[...] = frame[rows : 2 * rows]
    r = times_table(frame[...], cf[0], cf[1])
    r = row_spectrum(rf[0], rf[1], r)
    mixed = []
    for i in range(planes):
        h = [optic[i, j] for j in range(4)]
        g = (
            h[0] * r[0] + h[1] * r[1],
            h[0] * r[1] - h[1] * r[0],
            h[2] * r[2] + h[3] * r[3],
            h[2] * r[3] - h[3] * r[2],
        )
        mixed.append(table_times(rt[0, :rows], rt[1, :rows], folded(g)))
    gradient = times_table(jnp.concatenate(mixed, axis=0), ct[0], ct[1])
    shifted = volume[...] - step_size * gradient.reshape(planes, rows, width)
    volume_next[...] = jnp.maximum(shifted - threshold, 0.0) + jnp.minimum(
        shifted + threshold, 0.0
    )


def swap(x, axis, mask):
    return lax.ppermute(x, axis, [(i, i ^ mask) for i in range(lax.axis_size(axis))])


def pairing(depths, tiles, start):
    partner = {}
    for t in range(tiles):
        other = t + 1 if (t - start) % 2 == 0 else t - 1
        for d in range(depths):
            inside = 0 <= other < tiles
            partner[d * tiles + t] = d * tiles + other if inside else (d ^ 1) * tiles + t
    return sorted(partner.items())


def local(kernel, name, outs, *args):
    return pl.pallas_call(
        kernel,
        out_shape=[pltpu.VMEM(x, jnp.float32) for x in outs],
        in_specs=[VMEM] * len(args),
        out_specs=[VMEM] * len(outs),
        compiler_params=SMALL,
        name=name,
    )(*args)


def in_hbm(x):
    return pltpu.with_memory_space_constraint(x, pltpu.HBM)


def per_device(volume, point_spread, measured):
    planes, rows, width = volume.shape
    half_width = (point_spread.shape[1] - 1) // 2
    n = lax.axis_size("depth")
    tiles = lax.axis_size("tile")
    chips = n // 2
    f32, bf16 = jnp.float32, jnp.bfloat16
    rf, cf, shift = (jnp.asarray(x) for x in tables(rows, width, half_width))
    u, v = rf.shape[1], cf.shape[2]
    piece = (rows // 2, width)
    three = (3,) + piece
    kp = -(-(rows + half_width + 1) // 128) * 128
    spread = jnp.transpose(point_spread, (1, 0, 2))
    operands = (volume, spread, rf, cf, shift, measured)
    keep, send, optic, rf, rt, cf, ct = pl.pallas_call(
        project_kernel,
        out_shape=[
            pltpu.VMEM(three, f32),
            pltpu.VMEM(three, f32),
            pltpu.VMEM((planes, 4, u // 2, v // 2), f32),
            pltpu.VMEM(rf.shape, bf16),
            pltpu.VMEM((2, rf.shape[2], u), bf16),
            pltpu.VMEM(cf.shape, bf16),
            pltpu.VMEM((2, v, width), bf16),
        ],
        in_specs=[HBM] * 6,
        out_specs=[VMEM] * 7,
        scratch_shapes=[
            pltpu.VMEM(volume.shape, f32),
            pltpu.VMEM(spread.shape, f32),
            pltpu.VMEM(shift.shape, f32),
            pltpu.VMEM(measured.shape, f32),
            pltpu.VMEM((planes, kp, kp), f32),
            pltpu.SemaphoreType.DMA((7,)),
        ],
        compiler_params=PARAMS,
        name="project",
    )(*[in_hbm(x) for x in operands])
    received = swap(send, "depth", 1)
    pairs = [pairing(n, tiles, start) for start in (0, 1)]
    own, *sends = local(split_kernel, "split", [piece] * 3, keep, received)
    beside = [lax.ppermute(x, ("depth", "tile"), p) for x, p in zip(sends, pairs)]
    (part,) = local(tile_sum_kernel, "sum_tiles", [piece], own, *beside)
    others = [swap(part, "depth", 2 * m) for m in range(1, chips)]
    (whole,) = local(sum_kernel, "sum_chips", [piece], part, *others)
    beside = [lax.ppermute(whole, ("depth", "tile"), p) for p in pairs[::-1]]
    (gathered,) = local(stack_kernel, "stack", [three], whole, *beside)
    other = swap(gathered, "depth", 1)
    volume_next, residual = pl.pallas_call(
        back_kernel,
        out_shape=[
            jax.ShapeDtypeStruct(volume.shape, f32),
            jax.ShapeDtypeStruct(measured.shape, f32),
        ],
        in_specs=[VMEM] * 8,
        out_specs=[VMEM] * 2,
        scratch_shapes=[pltpu.VMEM((3 * rows, width), f32)],
        compiler_params=PARAMS,
        name="back",
    )(volume, gathered, other, optic, rf, rt, cf, ct)
    return volume_next, residual


def solution(mesh):
    placed = (P("depth", "tile", None), P("depth", None, None), P("tile", None))
    return jax.shard_map(
        per_device,
        mesh=mesh,
        in_specs=placed,
        out_specs=(P("depth", "tile", None), P("tile", None)),
        check_vma=False,
    )
```

```python
import jax
import jax.numpy as jnp
import ml_dtypes
import numpy as np
from jax import lax
from jax.experimental import pallas as pl
from jax.experimental.pallas import tpu as pltpu
from jax.sharding import PartitionSpec as P

step_size = 2.0
threshold = 0.5
VMEM = pl.BlockSpec(memory_space=pltpu.VMEM)
HBM = pl.BlockSpec(memory_space=pltpu.HBM)
PARAMS = pltpu.CompilerParams(vmem_limit_bytes=24 * 1024 * 1024)
SMALL = pltpu.CompilerParams(vmem_limit_bytes=4 * 1024 * 1024)


def pair(table):
    high = table.astype(ml_dtypes.bfloat16)
    low = (table - high.astype(np.float64)).astype(ml_dtypes.bfloat16)
    return np.stack([high, low])


def tables(row_count, width_count, half_width):
    freq_rows = 3 * row_count
    freq_cols = -(-(width_count + half_width) // 256) * 256
    row_angle = 2.0 * np.pi / freq_rows * (np.arange(freq_rows // 2) + 0.5)
    col_angle = 2.0 * np.pi / freq_cols * (np.arange(freq_cols // 2) + 0.5)
    row_phase = row_angle[:, None] * np.arange(freq_rows)[None, :]
    col_phase = np.arange(width_count)[:, None] * col_angle[None, :]
    row_table = np.concatenate([np.cos(row_phase), np.sin(row_phase)], axis=0)
    col_table = np.concatenate([np.cos(col_phase), -np.sin(col_phase)], axis=1)
    centre = np.stack([np.cos(half_width * col_angle), np.sin(half_width * col_angle)])
    shift = np.zeros((8, freq_cols // 2), np.float32)
    shift[:2] = centre * (2.0 / (freq_rows * freq_cols))
    return pair(row_table), pair(col_table), shift


def split(x):
    high = x.astype(jnp.bfloat16)
    low = (x - high.astype(jnp.float32)).astype(jnp.bfloat16)
    return high, low


def times_table(x, high, low):
    x_high, x_low = split(x)
    return jnp.dot(
        jnp.concatenate([x_high, x_low, x_high], axis=1),
        jnp.concatenate([high, high, low], axis=0),
        preferred_element_type=jnp.float32,
    )


def table_times(high, low, x):
    x_high, x_low = split(x)
    return jnp.dot(
        jnp.concatenate([high, high, low], axis=1),
        jnp.concatenate([x_high, x_low, x_high], axis=0),
        preferred_element_type=jnp.float32,
    )


def row_terms(q):
    u, v = q.shape[0] // 2, q.shape[1] // 2
    cr, ci, sr, si = q[:u, :v], q[:u, v:], q[u:, :v], q[u:, v:]
    return cr + si, ci - sr, cr - si, ci + sr


def row_spectrum(high, low, x):
    return row_terms(table_times(high, low, x))


def folded(spectrum):
    pr, pi, mr, mi = spectrum
    top = jnp.concatenate([pr + mr, pi + mi], axis=1)
    bottom = jnp.concatenate([mi - pi, pr - mr], axis=1)
    return jnp.concatenate([top, bottom], axis=0)


def project_kernel(
    volume_h,
    point_spread_h,
    rf_h,
    cf_h,
    shift_h,
    measured_h,
    spectrum,
    send,
    measured,
    optic,
    rf,
    rt,
    cf,
    ct,
    volume,
    point_spread,
    shift,
    pad,
    arrived,
):
    kp = pad.shape[1]
    moves = {}
    order = (
        ("spread", point_spread_h, point_spread),
        ("cf", cf_h.at[:, :kp], cf.at[:, :kp]),
        ("shift", shift_h, shift),
        ("rf", rf_h, rf),
        ("volume", volume_h, volume),
        ("cf_rest", cf_h.at[:, kp:], cf.at[:, kp:]),
        ("measured", measured_h, measured),
    )
    for i, (name, source, target) in enumerate(order):
        moves[name] = pltpu.make_async_copy(source, target, arrived.at[i])
        moves[name].start()
    planes, rows, width = volume.shape
    k = point_spread.shape[0]
    above = rows - (k - 1) // 2
    pad[...] = jnp.zeros_like(pad)
    moves["spread"].wait()
    for i in range(planes):
        pad[i, above : above + k, :k] = point_spread[:, i, :]
    moves["cf"].wait()
    moves["shift"].wait()
    cos, sin = shift[0:1], shift[1:2]
    v = cos.shape[1]
    x = times_table(pad[...].reshape(planes * kp, kp), cf[0, :kp], cf[1, :kp])
    re, im = x[:, :v], x[:, v:]
    spread = jnp.concatenate([re * cos - im * sin, re * sin + im * cos], axis=1)
    moves["volume"].wait()
    moves["cf_rest"].wait()
    image = times_table(volume[...].reshape(planes * rows, width), cf[0], cf[1])
    for i in range(2):
        ct[i] = cf[i].T
    moves["rf"].wait()
    rt[0] = rf[0].T
    rt[1] = rf[1].T
    total = None
    for i in range(planes):
        h = row_spectrum(rf[0, :, :kp], rf[1, :, :kp], spread[i * kp : (i + 1) * kp])
        for j in range(4):
            optic[i, j] = h[j]
        f = row_spectrum(rf[0, :, :rows], rf[1, :, :rows], image[i * rows : (i + 1) * rows])
        term = (
            h[0] * f[0] - h[1] * f[1],
            h[0] * f[1] + h[1] * f[0],
            h[2] * f[2] - h[3] * f[3],
            h[2] * f[3] + h[3] * f[2],
        )
        total = term if total is None else [a + b for a, b in zip(total, term)]
    spectrum[0], spectrum[1] = split(folded(total))
    image = image_rows(spectrum, rt, ct, 1)
    moves["measured"].wait()
    finish(image, measured, send, 1)


def image_rows(spectrum, rt, ct, other):
    rows = rt.shape[1] // 3
    half = rows // 2
    start = ((lax.axis_index("depth") + other) % 2) * half
    table = [
        jnp.concatenate(
            [rt[i, pl.ds(pl.multiple_of(s * rows + start, half), half)] for s in range(3)], axis=0
        )
        for i in range(2)
    ]
    mixed = jnp.dot(
        jnp.concatenate([table[0], table[0], table[1]], axis=1),
        jnp.concatenate([spectrum[0], spectrum[1], spectrum[0]], axis=0),
        preferred_element_type=jnp.float32,
    )
    return times_table(mixed, ct[0], ct[1])


def finish(image, measured, out, other):
    half = out.shape[1]
    d, t = lax.axis_index("depth"), lax.axis_index("tile")
    tiles = lax.axis_size("tile")
    seen = jnp.where((d + other) % 2 == 0, measured[:half], measured[half:])
    out[0] = image[:half] * jnp.where(t == 0, 0.0, 1.0)
    out[1] = image[half : 2 * half] - seen * jnp.where(d == 0, 1.0, 0.0)
    out[2] = image[2 * half :] * jnp.where(t == tiles - 1, 0.0, 1.0)


def keep_kernel(spectrum, rt, ct, measured, keep):
    finish(image_rows(spectrum, rt, ct, 0), measured, keep, 0)


def split_kernel(keep, received, own, first, second):
    even = lax.axis_index("tile") % 2 == 0
    up, down = keep[0] + received[0], keep[2] + received[2]
    own[...] = keep[1] + received[1]
    first[...] = jnp.where(even, down, up)
    second[...] = jnp.where(even, up, down)


def tree(terms):
    if len(terms) == 1:
        return terms[0]
    middle = len(terms) // 2
    return tree(terms[:middle]) + tree(terms[middle:])


def paired():
    t, n = lax.axis_index("tile"), lax.axis_size("tile")
    even = t % 2 == 0
    first = jnp.where(even, t + 1, t - 1)
    second = jnp.where(even, t - 1, t + 1)
    return first < n, jnp.logical_and(second >= 0, second < n)


def tile_sum_kernel(own, a, b, out):
    first, second = paired()
    out[...] = own[...] + jnp.where(first, a[...], 0.0) + jnp.where(second, b[...], 0.0)


def sum_kernel(*refs):
    refs[-1][...] = tree([x[...] for x in refs[:-1]])


def stack_kernel(*refs):
    for m, x in enumerate(refs[:-1]):
        refs[-1][m] = x[...]


def by_core(x):
    half = x.shape[-1] // 6
    even = lax.axis_index("depth") % 2 == 0
    first, second = (
        jnp.concatenate(
            [x[..., (2 * s + j) * half : (2 * s + j + 1) * half] for s in range(3)], axis=-1
        )
        for j in (0, 1)
    )
    return jnp.where(even, first, second), jnp.where(even, second, first)


def row_part(strips, table, cf):
    even = lax.axis_index("tile") % 2 == 0
    first, second = paired()
    b, a = jnp.where(second, strips[1], 0.0), jnp.where(first, strips[2], 0.0)
    x = jnp.concatenate([jnp.where(even, b, a), strips[0], jnp.where(even, a, b)], axis=0)
    return table_times(table[0], table[1], times_table(x, cf[0], cf[1]))


def near_kernel(mine, rf, cf, partial, other_table):
    tables = [by_core(rf[i]) for i in range(2)]
    partial[...] = row_part(mine, [x for x, _ in tables], cf)
    for i in range(2):
        other_table[i] = tables[i][1]


def back_kernel(volume, mine, other, table, partial, optic, rt, cf, ct, volume_next, residual):
    planes, rows, width = volume.shape
    half = rows // 2
    even = lax.axis_index("depth") % 2 == 0
    residual[:half] = jnp.where(even, mine[0], other[0])
    residual[half:] = jnp.where(even, other[0], mine[0])
    r = row_terms(partial[...] + row_part(other, table, cf))
    mixed = []
    for i in range(planes):
        h = [optic[i, j] for j in range(4)]
        g = (
            h[0] * r[0] + h[1] * r[1],
            h[0] * r[1] - h[1] * r[0],
            h[2] * r[2] + h[3] * r[3],
            h[2] * r[3] - h[3] * r[2],
        )
        mixed.append(table_times(rt[0, :rows], rt[1, :rows], folded(g)))
    gradient = times_table(jnp.concatenate(mixed, axis=0), ct[0], ct[1])
    shifted = volume[...] - step_size * gradient.reshape(planes, rows, width)
    volume_next[...] = jnp.maximum(shifted - threshold, 0.0) + jnp.minimum(
        shifted + threshold, 0.0
    )


def swap(x, axis, mask):
    return lax.ppermute(x, axis, [(i, i ^ mask) for i in range(lax.axis_size(axis))])


def pairing(depths, tiles, start):
    partner = {}
    for t in range(tiles):
        other = t + 1 if (t - start) % 2 == 0 else t - 1
        for d in range(depths):
            inside = 0 <= other < tiles
            partner[d * tiles + t] = d * tiles + other if inside else (d ^ 1) * tiles + t
    return sorted(partner.items())


def local(kernel, name, outs, *args):
    return pl.pallas_call(
        kernel,
        out_shape=[pltpu.VMEM(x, jnp.float32) for x in outs],
        in_specs=[VMEM] * len(args),
        out_specs=[VMEM] * len(outs),
        compiler_params=SMALL,
        name=name,
    )(*args)


def cost(flops):
    return pl.CostEstimate(flops=flops, bytes_accessed=0, transcendentals=0)


def in_hbm(x):
    return pltpu.with_memory_space_constraint(x, pltpu.HBM)


def per_device(volume, point_spread, measured):
    planes, rows, width = volume.shape
    half_width = (point_spread.shape[1] - 1) // 2
    n = lax.axis_size("depth")
    tiles = lax.axis_size("tile")
    chips = n // 2
    f32, bf16 = jnp.float32, jnp.bfloat16
    rf, cf, shift = (jnp.asarray(x) for x in tables(rows, width, half_width))
    u, v = rf.shape[1], cf.shape[2]
    piece = (rows // 2, width)
    three = (3,) + piece
    kp = -(-(rows + half_width + 1) // 128) * 128
    spread = jnp.transpose(point_spread, (1, 0, 2))
    operands = (volume, spread, rf, cf, shift, measured)
    spectrum, send, seen, optic, rf, rt, cf, ct = pl.pallas_call(
        project_kernel,
        out_shape=[
            pltpu.VMEM((2, u, v), bf16),
            pltpu.VMEM(three, f32),
            pltpu.VMEM(measured.shape, f32),
            pltpu.VMEM((planes, 4, u // 2, v // 2), f32),
            pltpu.VMEM(rf.shape, bf16),
            pltpu.VMEM((2, rf.shape[2], u), bf16),
            pltpu.VMEM(cf.shape, bf16),
            pltpu.VMEM((2, v, width), bf16),
        ],
        in_specs=[HBM] * 6,
        out_specs=[VMEM] * 8,
        scratch_shapes=[
            pltpu.VMEM(volume.shape, f32),
            pltpu.VMEM(spread.shape, f32),
            pltpu.VMEM(shift.shape, f32),
            pltpu.VMEM((planes, kp, kp), f32),
            pltpu.SemaphoreType.DMA((7,)),
        ],
        compiler_params=PARAMS,
        name="project",
    )(*[in_hbm(x) for x in operands])
    received = swap(send, "depth", 1)
    (keep,) = pl.pallas_call(
        keep_kernel,
        out_shape=[pltpu.VMEM(three, f32)],
        in_specs=[VMEM] * 4,
        out_specs=[VMEM],
        compiler_params=PARAMS,
        cost_estimate=cost(9 * rows * v * (width + u)),
        name="keep",
    )(spectrum, rt, ct, seen)
    pairs = [pairing(n, tiles, start) for start in (0, 1)]
    own, *sends = local(split_kernel, "split", [piece] * 3, keep, received)
    beside = [lax.ppermute(x, ("depth", "tile"), p) for x, p in zip(sends, pairs)]
    (part,) = local(tile_sum_kernel, "sum_tiles", [piece], own, *beside)
    others = [swap(part, "depth", 2 * m) for m in range(1, chips)]
    (whole,) = local(sum_kernel, "sum_chips", [piece], part, *others)
    beside = [lax.ppermute(whole, ("depth", "tile"), p) for p in pairs[::-1]]
    (gathered,) = local(stack_kernel, "stack", [three], whole, *beside)
    other = swap(gathered, "depth", 1)
    partial, table = pl.pallas_call(
        near_kernel,
        out_shape=[pltpu.VMEM((u, v), f32), pltpu.VMEM((2, u, 3 * rows // 2), bf16)],
        in_specs=[VMEM] * 3,
        out_specs=[VMEM] * 2,
        compiler_params=PARAMS,
        cost_estimate=cost(2 * rows * v * 3 * (width + u)),
        name="near",
    )(gathered, rf, cf)
    volume_next, residual = pl.pallas_call(
        back_kernel,
        out_shape=[
            jax.ShapeDtypeStruct(volume.shape, f32),
            jax.ShapeDtypeStruct(measured.shape, f32),
        ],
        in_specs=[VMEM] * 9,
        out_specs=[VMEM] * 2,
        compiler_params=PARAMS,
        name="back",
    )(volume, gathered, other, table, partial, optic, rt, cf, ct)
    return volume_next, residual


def solution(mesh):
    placed = (P("depth", "tile", None), P("depth", None, None), P("tile", None))
    return jax.shard_map(
        per_device,
        mesh=mesh,
        in_specs=placed,
        out_specs=(P("depth", "tile", None), P("tile", None)),
        check_vma=False,
    )
```

```python
import jax
import jax.numpy as jnp
import ml_dtypes
import numpy as np
from jax import lax
from jax.experimental import pallas as pl
from jax.experimental.pallas import tpu as pltpu
from jax.sharding import PartitionSpec as P

step_size = 2.0
threshold = 0.5
VMEM = pl.BlockSpec(memory_space=pltpu.VMEM)
HBM = pl.BlockSpec(memory_space=pltpu.HBM)
PARAMS = pltpu.CompilerParams(vmem_limit_bytes=24 * 1024 * 1024)
SMALL = pltpu.CompilerParams(vmem_limit_bytes=4 * 1024 * 1024)


def pair(table):
    high = table.astype(ml_dtypes.bfloat16)
    low = (table - high.astype(np.float64)).astype(ml_dtypes.bfloat16)
    return np.stack([high, low])


def tables(row_count, width_count, half_width):
    freq_rows = 3 * row_count
    freq_cols = -(-(width_count + half_width) // 256) * 256
    row_angle = 2.0 * np.pi / freq_rows * (np.arange(freq_rows // 2) + 0.5)
    col_angle = 2.0 * np.pi / freq_cols * (np.arange(freq_cols // 2) + 0.5)
    row_phase = row_angle[:, None] * np.arange(freq_rows)[None, :]
    col_phase = np.arange(width_count)[:, None] * col_angle[None, :]
    row_table = np.concatenate([np.cos(row_phase), np.sin(row_phase)], axis=0)
    col_table = np.concatenate([np.cos(col_phase), -np.sin(col_phase)], axis=1)
    centre = np.stack([np.cos(half_width * col_angle), np.sin(half_width * col_angle)])
    shift = np.zeros((8, freq_cols // 2), np.float32)
    shift[:2] = centre * (2.0 / (freq_rows * freq_cols))
    return pair(row_table), pair(col_table), shift


def split(x):
    high = x.astype(jnp.bfloat16)
    low = (x - high.astype(jnp.float32)).astype(jnp.bfloat16)
    return high, low


def times_table(x, high, low):
    x_high, x_low = split(x)
    return jnp.dot(
        jnp.concatenate([x_high, x_low, x_high], axis=1),
        jnp.concatenate([high, high, low], axis=0),
        preferred_element_type=jnp.float32,
    )


def table_times(high, low, x):
    x_high, x_low = split(x)
    return jnp.dot(
        jnp.concatenate([high, high, low], axis=1),
        jnp.concatenate([x_high, x_low, x_high], axis=0),
        preferred_element_type=jnp.float32,
    )


def row_terms(q):
    u, v = q.shape[0] // 2, q.shape[1] // 2
    cr, ci, sr, si = q[:u, :v], q[:u, v:], q[u:, :v], q[u:, v:]
    return cr + si, ci - sr, cr - si, ci + sr


def row_spectrum(high, low, x):
    return row_terms(table_times(high, low, x))


def folded(spectrum):
    pr, pi, mr, mi = spectrum
    top = jnp.concatenate([pr + mr, pi + mi], axis=1)
    bottom = jnp.concatenate([mi - pi, pr - mr], axis=1)
    return jnp.concatenate([top, bottom], axis=0)


def project_kernel(
    volume_h,
    point_spread_h,
    rf_h,
    cf_h,
    shift_h,
    measured_h,
    spectrum,
    send,
    measured,
    optic,
    rf,
    rt,
    cf,
    ct,
    volume,
    point_spread,
    shift,
    pad,
    arrived,
):
    kp = pad.shape[1]
    moves = {}
    order = (
        ("spread", point_spread_h, point_spread),
        ("cf", cf_h.at[:, :kp], cf.at[:, :kp]),
        ("shift", shift_h, shift),
        ("rf", rf_h, rf),
        ("volume", volume_h, volume),
        ("cf_rest", cf_h.at[:, kp:], cf.at[:, kp:]),
        ("measured", measured_h, measured),
    )
    for i, (name, source, target) in enumerate(order):
        moves[name] = pltpu.make_async_copy(source, target, arrived.at[i])
        moves[name].start()
    planes, rows, width = volume.shape
    k = point_spread.shape[0]
    above = rows - (k - 1) // 2
    pad[...] = jnp.zeros_like(pad)
    moves["spread"].wait()
    for i in range(planes):
        pad[i, above : above + k, :k] = point_spread[:, i, :]
    moves["cf"].wait()
    moves["shift"].wait()
    cos, sin = shift[0:1], shift[1:2]
    v = cos.shape[1]
    x = times_table(pad[...].reshape(planes * kp, kp), cf[0, :kp], cf[1, :kp])
    re, im = x[:, :v], x[:, v:]
    spread = jnp.concatenate([re * cos - im * sin, re * sin + im * cos], axis=1)
    moves["volume"].wait()
    moves["cf_rest"].wait()
    image = times_table(volume[...].reshape(planes * rows, width), cf[0], cf[1])
    for i in range(2):
        ct[i] = cf[i].T
    moves["rf"].wait()
    rt[0] = rf[0].T
    rt[1] = rf[1].T
    total = None
    for i in range(planes):
        h = row_spectrum(rf[0, :, :kp], rf[1, :, :kp], spread[i * kp : (i + 1) * kp])
        for j in range(4):
            optic[i, j] = h[j]
        f = row_spectrum(rf[0, :, :rows], rf[1, :, :rows], image[i * rows : (i + 1) * rows])
        term = (
            h[0] * f[0] - h[1] * f[1],
            h[0] * f[1] + h[1] * f[0],
            h[2] * f[2] - h[3] * f[3],
            h[2] * f[3] + h[3] * f[2],
        )
        total = term if total is None else [a + b for a, b in zip(total, term)]
    spectrum[0], spectrum[1] = split(folded(total))
    image = image_rows(spectrum, rt, ct, 1)
    moves["measured"].wait()
    finish(image, measured, send, 1)


def image_rows(spectrum, rt, ct, other):
    rows = rt.shape[1] // 3
    half = rows // 2
    start = ((lax.axis_index("depth") + other) % 2) * half
    table = [
        jnp.concatenate(
            [rt[i, pl.ds(pl.multiple_of(s * rows + start, half), half)] for s in range(3)], axis=0
        )
        for i in range(2)
    ]
    mixed = jnp.dot(
        jnp.concatenate([table[0], table[0], table[1]], axis=1),
        jnp.concatenate([spectrum[0], spectrum[1], spectrum[0]], axis=0),
        preferred_element_type=jnp.float32,
    )
    return times_table(mixed, ct[0], ct[1])


def finish(image, measured, out, other):
    half = out.shape[1]
    d, t = lax.axis_index("depth"), lax.axis_index("tile")
    tiles = lax.axis_size("tile")
    seen = jnp.where((d + other) % 2 == 0, measured[:half], measured[half:])
    out[0] = image[:half] * jnp.where(t == 0, 0.0, 1.0)
    out[1] = image[half : 2 * half] - seen * jnp.where(d == 0, 1.0, 0.0)
    out[2] = image[2 * half :] * jnp.where(t == tiles - 1, 0.0, 1.0)


def keep_kernel(spectrum, rt, ct, measured, keep):
    finish(image_rows(spectrum, rt, ct, 0), measured, keep, 0)


def split_kernel(keep, received, own, first, second):
    even = lax.axis_index("tile") % 2 == 0
    up, down = keep[0] + received[0], keep[2] + received[2]
    own[...] = keep[1] + received[1]
    first[...] = jnp.where(even, down, up)
    second[...] = jnp.where(even, up, down)


def tree(terms):
    if len(terms) == 1:
        return terms[0]
    middle = len(terms) // 2
    return tree(terms[:middle]) + tree(terms[middle:])


def paired():
    t, n = lax.axis_index("tile"), lax.axis_size("tile")
    even = t % 2 == 0
    first = jnp.where(even, t + 1, t - 1)
    second = jnp.where(even, t - 1, t + 1)
    return first < n, jnp.logical_and(second >= 0, second < n)


def tile_sum_kernel(own, a, b, out):
    first, second = paired()
    out[...] = own[...] + jnp.where(first, a[...], 0.0) + jnp.where(second, b[...], 0.0)


def sum_kernel(*refs):
    refs[-1][...] = tree([x[...] for x in refs[:-1]])


def stack_kernel(whole, whole_other, b, a, mine, halo):
    for m, x in enumerate((whole, whole_other, b, a)):
        mine[m] = x[...]
    halo[0] = b[...]
    halo[1] = a[...]


def beside_first(b, a):
    even = lax.axis_index("tile") % 2 == 0
    first, second = paired()
    b, a = jnp.where(second, b, 0.0), jnp.where(first, a, 0.0)
    return jnp.concatenate([jnp.where(even, b, a), jnp.where(even, a, b)], axis=0)


def own_strip(whole, whole_other):
    even = lax.axis_index("depth") % 2 == 0
    return jnp.concatenate(
        [jnp.where(even, whole, whole_other), jnp.where(even, whole_other, whole)], axis=0
    )


def by_core(x):
    rows = x.shape[-1] // 3
    half = rows // 2
    even = lax.axis_index("depth") % 2 == 0
    above, below = x[..., :rows], x[..., 2 * rows :]
    first = jnp.concatenate([above[..., :half], below[..., :half]], axis=-1)
    second = jnp.concatenate([above[..., half:], below[..., half:]], axis=-1)
    return jnp.where(even, first, second), jnp.where(even, second, first)


def near_kernel(mine, rf, cf, partial, other_table):
    rows = rf.shape[2] // 3
    tables = [by_core(rf[i]) for i in range(2)]
    table = [
        jnp.concatenate([rf[i, :, rows : 2 * rows], tables[i][0]], axis=1) for i in range(2)
    ]
    x = jnp.concatenate([own_strip(mine[0], mine[1]), beside_first(mine[2], mine[3])], axis=0)
    partial[...] = table_times(table[0], table[1], times_table(x, cf[0], cf[1]))
    for i in range(2):
        other_table[i] = tables[i][1]


def back_kernel(volume, mine, other, table, partial, optic, rt, cf, ct, volume_next, residual):
    planes, rows, width = volume.shape
    residual[...] = own_strip(mine[0], mine[1])
    x = times_table(beside_first(other[0], other[1]), cf[0], cf[1])
    r = row_terms(partial[...] + table_times(table[0], table[1], x))
    mixed = []
    for i in range(planes):
        h = [optic[i, j] for j in range(4)]
        g = (
            h[0] * r[0] + h[1] * r[1],
            h[0] * r[1] - h[1] * r[0],
            h[2] * r[2] + h[3] * r[3],
            h[2] * r[3] - h[3] * r[2],
        )
        mixed.append(table_times(rt[0, :rows], rt[1, :rows], folded(g)))
    gradient = times_table(jnp.concatenate(mixed, axis=0), ct[0], ct[1])
    shifted = volume[...] - step_size * gradient.reshape(planes, rows, width)
    volume_next[...] = jnp.maximum(shifted - threshold, 0.0) + jnp.minimum(
        shifted + threshold, 0.0
    )


def swap(x, axis, mask):
    return lax.ppermute(x, axis, [(i, i ^ mask) for i in range(lax.axis_size(axis))])


def pairing(depths, tiles, start):
    partner = {}
    for t in range(tiles):
        other = t + 1 if (t - start) % 2 == 0 else t - 1
        for d in range(depths):
            inside = 0 <= other < tiles
            partner[d * tiles + t] = d * tiles + other if inside else (d ^ 1) * tiles + t
    return sorted(partner.items())


def local(kernel, name, outs, *args):
    return pl.pallas_call(
        kernel,
        out_shape=[pltpu.VMEM(x, jnp.float32) for x in outs],
        in_specs=[VMEM] * len(args),
        out_specs=[VMEM] * len(outs),
        compiler_params=SMALL,
        name=name,
    )(*args)


def cost(flops):
    return pl.CostEstimate(flops=flops, bytes_accessed=0, transcendentals=0)


def in_hbm(x):
    return pltpu.with_memory_space_constraint(x, pltpu.HBM)


def per_device(volume, point_spread, measured):
    planes, rows, width = volume.shape
    half_width = (point_spread.shape[1] - 1) // 2
    n = lax.axis_size("depth")
    tiles = lax.axis_size("tile")
    chips = n // 2
    f32, bf16 = jnp.float32, jnp.bfloat16
    rf, cf, shift = (jnp.asarray(x) for x in tables(rows, width, half_width))
    u, v = rf.shape[1], cf.shape[2]
    piece = (rows // 2, width)
    three = (3,) + piece
    kp = -(-(rows + half_width + 1) // 128) * 128
    spread = jnp.transpose(point_spread, (1, 0, 2))
    operands = (volume, spread, rf, cf, shift, measured)
    spectrum, send, seen, optic, rf, rt, cf, ct = pl.pallas_call(
        project_kernel,
        out_shape=[
            pltpu.VMEM((2, u, v), bf16),
            pltpu.VMEM(three, f32),
            pltpu.VMEM(measured.shape, f32),
            pltpu.VMEM((planes, 4, u // 2, v // 2), f32),
            pltpu.VMEM(rf.shape, bf16),
            pltpu.VMEM((2, rf.shape[2], u), bf16),
            pltpu.VMEM(cf.shape, bf16),
            pltpu.VMEM((2, v, width), bf16),
        ],
        in_specs=[HBM] * 6,
        out_specs=[VMEM] * 8,
        scratch_shapes=[
            pltpu.VMEM(volume.shape, f32),
            pltpu.VMEM(spread.shape, f32),
            pltpu.VMEM(shift.shape, f32),
            pltpu.VMEM((planes, kp, kp), f32),
            pltpu.SemaphoreType.DMA((7,)),
        ],
        compiler_params=PARAMS,
        name="project",
    )(*[in_hbm(x) for x in operands])
    received = swap(send, "depth", 1)
    (keep,) = pl.pallas_call(
        keep_kernel,
        out_shape=[pltpu.VMEM(three, f32)],
        in_specs=[VMEM] * 4,
        out_specs=[VMEM],
        compiler_params=PARAMS,
        cost_estimate=cost(9 * rows * v * (width + u)),
        name="keep",
    )(spectrum, rt, ct, seen)
    pairs = [pairing(n, tiles, start) for start in (0, 1)]
    own, *sends = local(split_kernel, "split", [piece] * 3, keep, received)
    beside = [lax.ppermute(x, ("depth", "tile"), p) for x, p in zip(sends, pairs)]
    (part,) = local(tile_sum_kernel, "sum_tiles", [piece], own, *beside)
    others = [swap(part, "depth", 2 * m) for m in range(1, chips)]
    (whole,) = local(sum_kernel, "sum_chips", [piece], part, *others)
    beside = [lax.ppermute(whole, ("depth", "tile"), p) for p in pairs[::-1]]
    whole_other = swap(whole, "depth", 1)
    gathered, halo = local(
        stack_kernel, "stack", [(4,) + piece, (2,) + piece], whole, whole_other, *beside
    )
    other = swap(halo, "depth", 1)
    partial, table = pl.pallas_call(
        near_kernel,
        out_shape=[pltpu.VMEM((u, v), f32), pltpu.VMEM((2, u, rows), bf16)],
        in_specs=[VMEM] * 3,
        out_specs=[VMEM] * 2,
        compiler_params=PARAMS,
        cost_estimate=cost(2 * rows * v * 3 * (width + u)),
        name="near",
    )(gathered, rf, cf)
    volume_next, residual = pl.pallas_call(
        back_kernel,
        out_shape=[
            jax.ShapeDtypeStruct(volume.shape, f32),
            jax.ShapeDtypeStruct(measured.shape, f32),
        ],
        in_specs=[VMEM] * 9,
        out_specs=[VMEM] * 2,
        compiler_params=PARAMS,
        name="back",
    )(volume, gathered, other, table, partial, optic, rt, cf, ct)
    return volume_next, residual


def solution(mesh):
    placed = (P("depth", "tile", None), P("depth", None, None), P("tile", None))
    return jax.shard_map(
        per_device,
        mesh=mesh,
        in_specs=placed,
        out_specs=(P("depth", "tile", None), P("tile", None)),
        check_vma=False,
    )
```

```python
import jax
import jax.numpy as jnp
import ml_dtypes
import numpy as np
from jax import lax
from jax.experimental import pallas as pl
from jax.experimental.pallas import tpu as pltpu
from jax.sharding import PartitionSpec as P

step_size = 2.0
threshold = 0.5
VMEM = pl.BlockSpec(memory_space=pltpu.VMEM)
HBM = pl.BlockSpec(memory_space=pltpu.HBM)
PARAMS = pltpu.CompilerParams(vmem_limit_bytes=24 * 1024 * 1024)
SMALL = pltpu.CompilerParams(vmem_limit_bytes=4 * 1024 * 1024)


def pair(table):
    high = table.astype(ml_dtypes.bfloat16)
    low = (table - high.astype(np.float64)).astype(ml_dtypes.bfloat16)
    return np.stack([high, low])


def tables(row_count, width_count, half_width):
    freq_rows = 3 * row_count
    freq_cols = -(-(width_count + half_width) // 256) * 256
    row_angle = 2.0 * np.pi / freq_rows * (np.arange(freq_rows // 2) + 0.5)
    col_angle = 2.0 * np.pi / freq_cols * (np.arange(freq_cols // 2) + 0.5)
    row_phase = row_angle[:, None] * np.arange(freq_rows)[None, :]
    col_phase = np.arange(width_count)[:, None] * col_angle[None, :]
    row_table = np.concatenate([np.cos(row_phase), np.sin(row_phase)], axis=0)
    col_table = np.concatenate([np.cos(col_phase), -np.sin(col_phase)], axis=1)
    centre = np.stack([np.cos(half_width * col_angle), np.sin(half_width * col_angle)])
    shift = np.zeros((8, freq_cols // 2), np.float32)
    shift[:2] = centre * (2.0 / (freq_rows * freq_cols))
    return pair(row_table), pair(col_table), shift


def split(x):
    high = x.astype(jnp.bfloat16)
    low = (x - high.astype(jnp.float32)).astype(jnp.bfloat16)
    return high, low


def times_table(x, high, low):
    x_high, x_low = split(x)
    return jnp.dot(
        jnp.concatenate([x_high, x_low, x_high], axis=1),
        jnp.concatenate([high, high, low], axis=0),
        preferred_element_type=jnp.float32,
    )


def table_times(high, low, x):
    x_high, x_low = split(x)
    return jnp.dot(
        jnp.concatenate([high, high, low], axis=1),
        jnp.concatenate([x_high, x_low, x_high], axis=0),
        preferred_element_type=jnp.float32,
    )


def row_terms(q):
    u, v = q.shape[0] // 2, q.shape[1] // 2
    cr, ci, sr, si = q[:u, :v], q[:u, v:], q[u:, :v], q[u:, v:]
    return cr + si, ci - sr, cr - si, ci + sr


def row_spectrum(high, low, x):
    return row_terms(table_times(high, low, x))


def folded(spectrum):
    pr, pi, mr, mi = spectrum
    top = jnp.concatenate([pr + mr, pi + mi], axis=1)
    bottom = jnp.concatenate([mi - pi, pr - mr], axis=1)
    return jnp.concatenate([top, bottom], axis=0)


def project_kernel(
    volume_h,
    point_spread_h,
    rf_h,
    cf_h,
    shift_h,
    measured_h,
    spectrum,
    send,
    measured,
    optic,
    rf,
    rt,
    cf,
    ct,
    volume,
    point_spread,
    shift,
    pad,
    arrived,
):
    kp = pad.shape[1]
    moves = {}
    order = (
        ("spread", point_spread_h, point_spread),
        ("cf", cf_h.at[:, :kp], cf.at[:, :kp]),
        ("shift", shift_h, shift),
        ("rf", rf_h, rf),
        ("volume", volume_h, volume),
        ("cf_rest", cf_h.at[:, kp:], cf.at[:, kp:]),
        ("measured", measured_h, measured),
    )
    for i, (name, source, target) in enumerate(order):
        moves[name] = pltpu.make_async_copy(source, target, arrived.at[i])
        moves[name].start()
    planes, rows, width = volume.shape
    k = point_spread.shape[0]
    above = rows - (k - 1) // 2
    pad[...] = jnp.zeros_like(pad)
    moves["spread"].wait()
    for i in range(planes):
        pad[i, above : above + k, :k] = point_spread[:, i, :]
    moves["cf"].wait()
    moves["shift"].wait()
    cos, sin = shift[0:1], shift[1:2]
    v = cos.shape[1]
    x = times_table(pad[...].reshape(planes * kp, kp), cf[0, :kp], cf[1, :kp])
    re, im = x[:, :v], x[:, v:]
    spread = jnp.concatenate([re * cos - im * sin, re * sin + im * cos], axis=1)
    moves["volume"].wait()
    moves["cf_rest"].wait()
    image = times_table(volume[...].reshape(planes * rows, width), cf[0], cf[1])
    for i in range(2):
        ct[i] = cf[i].T
    moves["rf"].wait()
    rt[0] = rf[0].T
    rt[1] = rf[1].T
    total = None
    for i in range(planes):
        h = row_spectrum(rf[0, :, :kp], rf[1, :, :kp], spread[i * kp : (i + 1) * kp])
        for j in range(4):
            optic[i, j] = h[j]
        f = row_spectrum(rf[0, :, :rows], rf[1, :, :rows], image[i * rows : (i + 1) * rows])
        term = (
            h[0] * f[0] - h[1] * f[1],
            h[0] * f[1] + h[1] * f[0],
            h[2] * f[2] - h[3] * f[3],
            h[2] * f[3] + h[3] * f[2],
        )
        total = term if total is None else [a + b for a, b in zip(total, term)]
    spectrum[0], spectrum[1] = split(folded(total))
    up, down = image_rows(spectrum, rt, ct, ((0, 1), (2, 1)))
    send[0], send[1] = seen_part(up, 0), seen_part(down, -1)
    moves["measured"].wait()


def seen_part(strip, edge):
    outside = edge % lax.axis_size("tile")
    return strip * jnp.where(lax.axis_index("tile") == outside, 0.0, 1.0)


def image_rows(spectrum, rt, ct, picks):
    rows = rt.shape[1] // 3
    half = rows // 2
    core = lax.axis_index("depth") % 2
    starts = [s * rows + (core + other) % 2 * half for s, other in picks]
    table = [
        jnp.concatenate([rt[i, pl.ds(pl.multiple_of(x, half), half)] for x in starts], axis=0)
        for i in range(2)
    ]
    mixed = jnp.dot(
        jnp.concatenate([table[0], table[0], table[1]], axis=1),
        jnp.concatenate([spectrum[0], spectrum[1], spectrum[0]], axis=0),
        preferred_element_type=jnp.float32,
    )
    image = times_table(mixed, ct[0], ct[1])
    return [image[j * half : (j + 1) * half] for j in range(len(picks))]


def keep_kernel(spectrum, rt, ct, measured, keep, own, own_send):
    half = own.shape[0]
    d = lax.axis_index("depth")
    up, down, mine, other = image_rows(spectrum, rt, ct, ((0, 0), (2, 0), (1, 0), (1, 1)))
    keep[0], keep[1] = seen_part(up, 0), seen_part(down, -1)
    once = jnp.where(d == 0, 1.0, 0.0)
    first, second = measured[:half] * once, measured[half:] * once
    own[...] = mine - jnp.where(d % 2 == 0, first, second)
    own_send[...] = other - jnp.where(d % 2 == 0, second, first)


def split_kernel(keep, received, first, second):
    even = lax.axis_index("tile") % 2 == 0
    up, down = keep[0] + received[0], keep[1] + received[1]
    first[...] = jnp.where(even, down, up)
    second[...] = jnp.where(even, up, down)


def tree(terms):
    if len(terms) == 1:
        return terms[0]
    middle = len(terms) // 2
    return tree(terms[:middle]) + tree(terms[middle:])


def paired():
    t, n = lax.axis_index("tile"), lax.axis_size("tile")
    even = t % 2 == 0
    first = jnp.where(even, t + 1, t - 1)
    second = jnp.where(even, t - 1, t + 1)
    return first < n, jnp.logical_and(second >= 0, second < n)


def tile_sum_kernel(own, a, b, own_received, out):
    first, second = paired()
    out[...] = own[...] + own_received[...] + jnp.where(first, a[...], 0.0) + jnp.where(second, b[...], 0.0)


def sum_kernel(*refs):
    refs[-1][...] = tree([x[...] for x in refs[:-1]])


def stack_kernel(whole, whole_other, b, a, mine, halo):
    for m, x in enumerate((whole, whole_other, b, a)):
        mine[m] = x[...]
    halo[0] = b[...]
    halo[1] = a[...]


def beside_first(b, a):
    even = lax.axis_index("tile") % 2 == 0
    first, second = paired()
    b, a = jnp.where(second, b, 0.0), jnp.where(first, a, 0.0)
    return jnp.concatenate([jnp.where(even, b, a), jnp.where(even, a, b)], axis=0)


def own_strip(whole, whole_other):
    even = lax.axis_index("depth") % 2 == 0
    return jnp.concatenate(
        [jnp.where(even, whole, whole_other), jnp.where(even, whole_other, whole)], axis=0
    )


def by_core(x):
    rows = x.shape[-1] // 3
    half = rows // 2
    even = lax.axis_index("depth") % 2 == 0
    above, below = x[..., :rows], x[..., 2 * rows :]
    first = jnp.concatenate([above[..., :half], below[..., :half]], axis=-1)
    second = jnp.concatenate([above[..., half:], below[..., half:]], axis=-1)
    return jnp.where(even, first, second), jnp.where(even, second, first)


def near_kernel(mine, rf, cf, partial, other_table):
    rows = rf.shape[2] // 3
    tables = [by_core(rf[i]) for i in range(2)]
    table = [
        jnp.concatenate([rf[i, :, rows : 2 * rows], tables[i][0]], axis=1) for i in range(2)
    ]
    x = jnp.concatenate([own_strip(mine[0], mine[1]), beside_first(mine[2], mine[3])], axis=0)
    partial[...] = table_times(table[0], table[1], times_table(x, cf[0], cf[1]))
    for i in range(2):
        other_table[i] = tables[i][1]


def back_kernel(volume, mine, other, table, partial, optic, rt, cf, ct, volume_next, residual):
    planes, rows, width = volume.shape
    residual[...] = own_strip(mine[0], mine[1])
    x = times_table(beside_first(other[0], other[1]), cf[0], cf[1])
    r = row_terms(partial[...] + table_times(table[0], table[1], x))
    mixed = []
    for i in range(planes):
        h = [optic[i, j] for j in range(4)]
        g = (
            h[0] * r[0] + h[1] * r[1],
            h[0] * r[1] - h[1] * r[0],
            h[2] * r[2] + h[3] * r[3],
            h[2] * r[3] - h[3] * r[2],
        )
        mixed.append(table_times(rt[0, :rows], rt[1, :rows], folded(g)))
    gradient = times_table(jnp.concatenate(mixed, axis=0), ct[0], ct[1])
    shifted = volume[...] - step_size * gradient.reshape(planes, rows, width)
    volume_next[...] = jnp.maximum(shifted - threshold, 0.0) + jnp.minimum(
        shifted + threshold, 0.0
    )


def swap(x, axis, mask):
    return lax.ppermute(x, axis, [(i, i ^ mask) for i in range(lax.axis_size(axis))])


def pairing(depths, tiles, start):
    partner = {}
    for t in range(tiles):
        other = t + 1 if (t - start) % 2 == 0 else t - 1
        for d in range(depths):
            inside = 0 <= other < tiles
            partner[d * tiles + t] = d * tiles + other if inside else (d ^ 1) * tiles + t
    return sorted(partner.items())


def local(kernel, name, outs, *args):
    return pl.pallas_call(
        kernel,
        out_shape=[pltpu.VMEM(x, jnp.float32) for x in outs],
        in_specs=[VMEM] * len(args),
        out_specs=[VMEM] * len(outs),
        compiler_params=SMALL,
        name=name,
    )(*args)


def cost(flops):
    return pl.CostEstimate(flops=flops, bytes_accessed=0, transcendentals=0)


def in_hbm(x):
    return pltpu.with_memory_space_constraint(x, pltpu.HBM)


def per_device(volume, point_spread, measured):
    planes, rows, width = volume.shape
    half_width = (point_spread.shape[1] - 1) // 2
    n = lax.axis_size("depth")
    tiles = lax.axis_size("tile")
    chips = n // 2
    f32, bf16 = jnp.float32, jnp.bfloat16
    rf, cf, shift = (jnp.asarray(x) for x in tables(rows, width, half_width))
    u, v = rf.shape[1], cf.shape[2]
    piece = (rows // 2, width)
    two = (2,) + piece
    kp = -(-(rows + half_width + 1) // 128) * 128
    spread = jnp.transpose(point_spread, (1, 0, 2))
    operands = (volume, spread, rf, cf, shift, measured)
    spectrum, send, seen, optic, rf, rt, cf, ct = pl.pallas_call(
        project_kernel,
        out_shape=[
            pltpu.VMEM((2, u, v), bf16),
            pltpu.VMEM(two, f32),
            pltpu.VMEM(measured.shape, f32),
            pltpu.VMEM((planes, 4, u // 2, v // 2), f32),
            pltpu.VMEM(rf.shape, bf16),
            pltpu.VMEM((2, rf.shape[2], u), bf16),
            pltpu.VMEM(cf.shape, bf16),
            pltpu.VMEM((2, v, width), bf16),
        ],
        in_specs=[HBM] * 6,
        out_specs=[VMEM] * 8,
        scratch_shapes=[
            pltpu.VMEM(volume.shape, f32),
            pltpu.VMEM(spread.shape, f32),
            pltpu.VMEM(shift.shape, f32),
            pltpu.VMEM((planes, kp, kp), f32),
            pltpu.SemaphoreType.DMA((7,)),
        ],
        compiler_params=PARAMS,
        name="project",
    )(*[in_hbm(x) for x in operands])
    received = swap(send, "depth", 1)
    keep, own, own_send = pl.pallas_call(
        keep_kernel,
        out_shape=[pltpu.VMEM(two, f32), pltpu.VMEM(piece, f32), pltpu.VMEM(piece, f32)],
        in_specs=[VMEM] * 4,
        out_specs=[VMEM] * 3,
        compiler_params=PARAMS,
        cost_estimate=cost(9 * rows * v * (width + u)),
        name="keep",
    )(spectrum, rt, ct, seen)
    pairs = [pairing(n, tiles, start) for start in (0, 1)]
    sends = local(split_kernel, "split", [piece] * 2, keep, received)
    own_send, *sends = lax.optimization_barrier((own_send, *sends))
    beside = [lax.ppermute(x, ("depth", "tile"), p) for x, p in zip(sends, pairs)]
    (part,) = local(tile_sum_kernel, "sum_tiles", [piece], own, *beside, swap(own_send, "depth", 1))
    others = [swap(part, "depth", 2 * m) for m in range(1, chips)]
    (whole,) = local(sum_kernel, "sum_chips", [piece], part, *others)
    beside = [lax.ppermute(whole, ("depth", "tile"), p) for p in pairs[::-1]]
    whole_other = swap(whole, "depth", 1)
    gathered, halo = local(
        stack_kernel, "stack", [(4,) + piece, two], whole, whole_other, *beside
    )
    other = swap(halo, "depth", 1)
    partial, table = pl.pallas_call(
        near_kernel,
        out_shape=[pltpu.VMEM((u, v), f32), pltpu.VMEM((2, u, rows), bf16)],
        in_specs=[VMEM] * 3,
        out_specs=[VMEM] * 2,
        compiler_params=PARAMS,
        cost_estimate=cost(2 * rows * v * 3 * (width + u)),
        name="near",
    )(gathered, rf, cf)
    volume_next, residual = pl.pallas_call(
        back_kernel,
        out_shape=[
            jax.ShapeDtypeStruct(volume.shape, f32),
            jax.ShapeDtypeStruct(measured.shape, f32),
        ],
        in_specs=[VMEM] * 9,
        out_specs=[VMEM] * 2,
        compiler_params=PARAMS,
        name="back",
    )(volume, gathered, other, table, partial, optic, rt, cf, ct)
    return volume_next, residual


def solution(mesh):
    placed = (P("depth", "tile", None), P("depth", None, None), P("tile", None))
    return jax.shard_map(
        per_device,
        mesh=mesh,
        in_specs=placed,
        out_specs=(P("depth", "tile", None), P("tile", None)),
        check_vma=False,
    )
```
